256 devices in a mesh: dp: 2 (over z_hi), seq: 32 (over x, y, core), head: 4 (over z_lo).
Axes of the slice: x: 4, y: 4, z: 8 (z_hi: 2, z_lo: 4; z = z_hi * 4 + z_lo), core: 2. Of those that a mesh axis runs over, the one named last changes fastest.
Arguments:
- queries: bfloat16 [32768, 3584], P(('dp', 'seq', 'head')), may hold values from -30 to 30
- keys: bfloat16 [32768, 512], P(('dp', 'seq', 'head')), may hold values from -5 to 5
- values: bfloat16 [32768, 512], P(('dp', 'seq', 'head')), may hold values from -6 to 6
- doc_lengths: int32 [2, 3], replicated, may hold values from 1 to 8192, 16384 in all within a row
- block_order: int32 [128], replicated, may hold values from 0 to 127, each once
Outputs:
- attended: bfloat16 [32768, 3584], P(('dp', 'seq', 'head'))
The draws below stay inside these ranges and needn't reach their ends.
Inputs may be any that keep to these rules, and one draw needn't show every extreme that they name: `doc_lengths`: each row sums to 16384, and its largest entry is exactly 8192. `block_order`: a permutation of the 128 global block numbers.
All inputs are finite; a program needn't handle non-finite values.
Results may differ from the reference program's by a relative error of at most 0.007.
Values may be sent and summed in bfloat16 or wider, within the bound.
No kernel may reach another device: no remote copies, remote signals or barrier semaphores. Data moves between devices by JAX's collectives and lax.ppermute only.
A program may use at most 64 MiB of HBM per device.

```python
import math
import jax
import jax.numpy as jnp
import numpy as np
from jax import lax

QUERY_HEADS = 28
KEY_VALUE_HEADS = 4
HEAD_WIDTH = 128
BLOCK_TOKENS = 256
DOCS = 3
GROUPS = 2
SEQ_LEN = 16384
MOST = 8192
NBLOCKS = 128
TOKEN_TOTAL = 32768


def draw_keys(key, part):
    key = jax.random.fold_in(key, 3)
    attention_output = jnp.clip(jax.random.normal(key, (TOKEN_TOTAL, KEY_VALUE_HEADS * HEAD_WIDTH), jnp.float32), -5.0, 5.0)
    return attention_output.astype(jnp.bfloat16)


def draw_queries(key, part):
    key = jax.random.fold_in(key, 5)
    attention_output = jnp.clip(jax.random.normal(key, (TOKEN_TOTAL, QUERY_HEADS * HEAD_WIDTH), jnp.float32), -5.0, 5.0)
    return attention_output.astype(jnp.bfloat16)


def levels(rng, extent, cuts, smallest, top_value):
    loudness, own = 1.0, jax.random.fold_in(rng, 6)
    for axis_at, shards_of in cuts:
        steps = jnp.exp(jax.random.uniform(jax.random.fold_in(own, axis_at), (shards_of,), jnp.float32, smallest / len(cuts), top_value / len(cuts)))
        loudness = loudness * jnp.repeat(steps, extent[axis_at] // shards_of).reshape([-1 if axis == axis_at else 1 for axis in range(len(extent))])
    return loudness


def split_up(count, total, bound, skew):
    weights = [(1 << 20) // math.isqrt(grade ** skew) + 1 for grade in range(2, count + 1)]
    rest, given = total - bound - (count - 1), [1] * (count - 1)
    while rest > 0:
        movable = [i for i in range(count - 1) if given[i] < bound]
        mass, remaining = sum([weights[i] for i in movable]), rest
        for i in movable:
            extra = min(bound - given[i], max(1, remaining * weights[i] // mass), rest)
            given[i] = given[i] + extra
            rest = rest - extra
    return np.array([bound] + given)


def uneven_parts(rng, amount, total, most, slope):
    if amount == 2:
        one = jax.random.randint(rng, (), max(1, total - most), min(most, total - 1) + 1)
        return jnp.stack([one, total - one])
    sizes = jnp.asarray(split_up(amount, total, most, slope), jnp.int32)
    twos = (amount - 1) // 2
    source_of, receiver = sizes[1:1 + 2 * twos:2], sizes[2:2 + 2 * twos:2]
    slack = jnp.minimum(source_of - 1, most - receiver)
    moved = jax.random.randint(jax.random.fold_in(rng, 1), (twos,), 0, 1 << 20) % (slack + 1)
    sizes = sizes.at[1:1 + 2 * twos:2].set(source_of - moved).at[2:2 + 2 * twos:2].set(receiver + moved)
    return sizes[jax.random.permutation(jax.random.fold_in(rng, 2), amount)]


def bell_draw(stream_key, extent, scale, bound, cuts=(), kind=jnp.bfloat16):
    values = scale * jax.random.normal(stream_key, extent, jnp.float32)
    if cuts:
        values = values * levels(stream_key, extent, cuts, -0.22, 0.18)
    return jnp.clip(values, -bound, bound).astype(kind)


def setup_inputs(seed: int = 0) -> dict:
    key_of = jax.random.split(jax.random.key(seed), 6)
    queries = draw_queries(jax.random.fold_in(key_of[5], 71), 0)
    keys = draw_keys(jax.random.fold_in(key_of[5], 71), 0)
    values = bell_draw(key_of[2], (TOKEN_TOTAL, KEY_VALUE_HEADS * HEAD_WIDTH), 1.0, 6.0, ((0, 256),))
    doc_lengths = jax.vmap(lambda own: uneven_parts(own, DOCS, SEQ_LEN, MOST, 2))(jax.random.split(key_of[3], GROUPS)).reshape((GROUPS, DOCS)).astype(jnp.int32)
    block_order = jax.random.permutation(key_of[4], NBLOCKS).astype(jnp.int32)
    return dict(queries=queries, keys=keys, values=values, doc_lengths=doc_lengths, block_order=block_order)


def attend_sequence(query_sequence, keys_seq, values_seq, labels):
    visible_span = MOST + BLOCK_TOKENS
    query_group_width = QUERY_HEADS // KEY_VALUE_HEADS
    padded_key_rows = jnp.concatenate([jnp.zeros((MOST, keys_seq.shape[1]), keys_seq.dtype), keys_seq])
    padded_value_rows = jnp.concatenate([jnp.zeros((MOST, values_seq.shape[1]), values_seq.dtype), values_seq])
    labels_padded = jnp.concatenate([jnp.full((MOST,), -1, jnp.int32), labels])
    scale = 1.0 / math.sqrt(HEAD_WIDTH)

    def one_block(block_index):
        first_row_index = (block_index * BLOCK_TOKENS).astype(jnp.int32)
        query_block = lax.dynamic_slice_in_dim(query_sequence, first_row_index, BLOCK_TOKENS, 0).astype(jnp.float32).reshape(BLOCK_TOKENS, KEY_VALUE_HEADS, query_group_width, HEAD_WIDTH)
        key_block = lax.dynamic_slice_in_dim(padded_key_rows, first_row_index, visible_span, 0).astype(jnp.float32).reshape(visible_span, KEY_VALUE_HEADS, HEAD_WIDTH)
        value_block = lax.dynamic_slice_in_dim(padded_value_rows, first_row_index, visible_span, 0).astype(jnp.float32).reshape(visible_span, KEY_VALUE_HEADS, HEAD_WIDTH)
        q_labels = lax.dynamic_slice_in_dim(labels, first_row_index, BLOCK_TOKENS, 0)
        k_labels = lax.dynamic_slice_in_dim(labels_padded, first_row_index, visible_span, 0)
        q_spots = first_row_index + jnp.arange(BLOCK_TOKENS, dtype=jnp.int32)
        k_spots = first_row_index - MOST + jnp.arange(visible_span, dtype=jnp.int32)
        allowed = (q_labels[:, None] == k_labels[None, :]) & (k_spots[None, :] <= q_spots[:, None])
        scores = jnp.einsum('qhgd,khd->hgqk', query_block, key_block) * scale
        scores = jnp.where(allowed[None, None], scores, -jnp.inf)
        row_max = lax.optimization_barrier(jnp.max(scores, axis=-1, keepdims=True))
        weights = jnp.exp(scores - row_max)
        totals = lax.optimization_barrier(jnp.sum(weights, axis=-1))
        rounded = lax.optimization_barrier(weights.astype(jnp.bfloat16)).astype(jnp.float32)
        numerator = jnp.einsum('hgqk,khd->qhgd', rounded, value_block)
        attention_output = numerator / jnp.transpose(totals, (2, 0, 1))[..., None]
        return attention_output.astype(jnp.bfloat16).reshape(BLOCK_TOKENS, QUERY_HEADS * HEAD_WIDTH)
    blocks_out = lax.map(one_block, jnp.arange(SEQ_LEN // BLOCK_TOKENS, dtype=jnp.int32))
    return blocks_out.reshape(SEQ_LEN, QUERY_HEADS * HEAD_WIDTH)

def reference(queries, keys, values, doc_lengths, block_order):
    block_count = block_order.shape[0]
    placing = jnp.zeros((block_count,), jnp.int32).at[block_order].set(jnp.arange(block_count, dtype=jnp.int32))

    def arrange(source):
        return source.reshape(block_count, BLOCK_TOKENS, source.shape[1])[placing].reshape(GROUPS, SEQ_LEN, source.shape[1])
    query_sequence = arrange(queries)
    keys_seq = arrange(keys)
    values_seq = arrange(values)
    doc_ends = jnp.cumsum(doc_lengths, axis=1).astype(jnp.int32)
    positions = jnp.arange(SEQ_LEN, dtype=jnp.int32)
    labels = lax.optimization_barrier(jnp.sum((positions[None, :, None] >= doc_ends[:, None, :]).astype(jnp.int32), axis=2))
    results = []
    for seq_group in range(GROUPS):
        results.append(attend_sequence(query_sequence[seq_group], keys_seq[seq_group], values_seq[seq_group], labels[seq_group]))
    global_out = jnp.stack(results).reshape(block_count, BLOCK_TOKENS, QUERY_HEADS * HEAD_WIDTH)
    return global_out[block_order].reshape(TOKEN_TOTAL, QUERY_HEADS * HEAD_WIDTH)
```

```python
import math

import jax
import jax.numpy as jnp
from jax import lax
from jax.experimental import pallas as pl
from jax.experimental.pallas import tpu as pltpu
from jax.sharding import PartitionSpec as P

HEAD_WIDTH = 128
ALL = ("dp", "seq", "head")
HEADS = 7
BLOCK = 256
SEQ_LEN = 16384
PER_SEQ = 64
MEMBERS = 32
STEP = 512
PAIRS = 4
SPAN = PAIRS * STEP
ROWS = 16
PAIR_ROWS = HEADS * ROWS
NEG = -1e30
SCALE = math.log2(math.e) / math.sqrt(HEAD_WIDTH)


def attend_tile(meta, q_ref, kv_ref, o_ref, stacked, peak, total):
    first = pl.program_id(0) * SPAN
    me = meta[2]
    ends = (meta[0], meta[1])
    for pair in range(PAIRS):
        for head in range(HEADS):
            at = pair * PAIR_ROWS + head * ROWS
            stacked[at : at + ROWS, :] = q_ref[
                pair * ROWS : (pair + 1) * ROWS, head * HEAD_WIDTH : (head + 1) * HEAD_WIDTH
            ]

    def start_of(position):
        return jnp.where(
            position >= ends[1], ends[1], jnp.where(position >= ends[0], ends[0], 0)
        )

    begin = start_of(first) // STEP
    diagonal = first // STEP
    clean = jnp.clip((start_of(first + SPAN - 1) + STEP - 1) // STEP, begin, diagonal)

    def spread(index):
        return (index // 8) * BLOCK + ((index // 4) % 2) * (BLOCK // 2) + index % 4

    row = lax.broadcasted_iota(jnp.int32, (PAIR_ROWS, 1), 0)
    column = lax.broadcasted_iota(jnp.int32, (1, STEP), 1)
    q_places = spread(row % ROWS) + 4 * me
    k_places = spread(column % ROWS) + 4 * (column // ROWS)
    peak[...] = jnp.full(peak.shape, NEG, jnp.float32)
    total[...] = jnp.zeros(total.shape, jnp.float32)
    ones = jnp.ones((STEP, HEAD_WIDTH), jnp.bfloat16)

    def absorb(step, from_pair, masked):
        block = kv_ref[:, pl.ds(pl.multiple_of(step * ROWS, ROWS), ROWS), :].reshape(
            STEP, 2 * HEAD_WIDTH
        )
        keys = block[:, :HEAD_WIDTH]
        values = jnp.concatenate([block[:, HEAD_WIDTH:], ones], axis=1)
        for pair in range(from_pair, PAIRS):
            rows = slice(pair * PAIR_ROWS, (pair + 1) * PAIR_ROWS)
            score = SCALE * lax.dot_general(
                stacked[rows, :], keys, (((1,), (1,)), ((), ())), preferred_element_type=jnp.float32
            )
            if masked:
                q_spots = q_places + (first + pair * STEP)
                k_spots = k_places + step * STEP
                seen = (k_spots >= start_of(q_spots)) & (k_spots <= q_spots)
                score = jnp.where(seen, score, NEG)
            before = peak[rows, :]
            now = jnp.maximum(before, jnp.max(score, axis=1, keepdims=True))
            peak[rows, :] = now
            fade = jnp.exp2(before - now)
            weight = jnp.exp2(score - jnp.concatenate([now] * (STEP // HEAD_WIDTH), axis=1))
            update = jnp.dot(
                weight.astype(jnp.bfloat16), values, preferred_element_type=jnp.float32
            )
            total[rows, :] = total[rows, :] * jnp.concatenate([fade] * 2, axis=1) + update

    @pl.loop(begin, clean)
    def _(step):
        absorb(step, 0, True)

    @pl.loop(clean, diagonal)
    def _(step):
        absorb(step, 0, False)

    for pair in range(PAIRS):
        absorb(diagonal + pair, pair, True)
    for pair in range(PAIRS):
        for head in range(HEADS):
            at = pair * PAIR_ROWS + head * ROWS
            mean = total[at : at + ROWS, :HEAD_WIDTH] / total[at : at + ROWS, HEAD_WIDTH:]
            o_ref[
                pair * ROWS : (pair + 1) * ROWS, head * HEAD_WIDTH : (head + 1) * HEAD_WIDTH
            ] = mean.astype(o_ref.dtype)


def attend(queries, keys_values, meta):
    rows, width = queries.shape
    tile_rows = PAIRS * ROWS
    return pl.pallas_call(
        attend_tile,
        out_shape=jax.ShapeDtypeStruct((rows, width), jnp.bfloat16),
        grid_spec=pltpu.PrefetchScalarGridSpec(
            num_scalar_prefetch=1,
            grid=(rows // tile_rows,),
            in_specs=[
                pl.BlockSpec((tile_rows, width), lambda i, m: (i, 0)),
                pl.BlockSpec(keys_values.shape, lambda i, m: (0, 0, 0)),
            ],
            out_specs=pl.BlockSpec((tile_rows, width), lambda i, m: (i, 0)),
            scratch_shapes=[
                pltpu.VMEM((PAIRS * PAIR_ROWS, HEAD_WIDTH), jnp.bfloat16),
                pltpu.VMEM((PAIRS * PAIR_ROWS, HEAD_WIDTH), jnp.float32),
                pltpu.VMEM((PAIRS * PAIR_ROWS, 2 * HEAD_WIDTH), jnp.float32),
            ],
        ),
        compiler_params=pltpu.CompilerParams(vmem_limit_bytes=48 * 1024 * 1024),
    )(meta, queries, keys_values)


def scatter_rows(rows):
    width = rows.shape[2]
    pieces = rows.reshape(MEMBERS, 4, 4, width).transpose(0, 2, 1, 3)
    both = jnp.broadcast_to(pieces[None], (2,) + pieces.shape).reshape(256, 4, width)
    return lax.all_to_all(both, ALL, split_axis=0, concat_axis=0, tiled=True)


def body(queries, keys, values, doc_lengths, block_order):
    tok_rows = queries.shape[0]
    sequence = lax.axis_index("dp")
    member = lax.axis_index("seq")
    place = lax.axis_index(ALL)
    ends = jnp.cumsum(doc_lengths, axis=1).astype(jnp.int32)
    my_ends = lax.dynamic_index_in_dim(ends, sequence, 0, keepdims=False)
    meta = jnp.stack([my_ends[0], my_ends[1], member]).astype(jnp.int32)

    source = jnp.arange(256 * 4, dtype=jnp.int32)
    target = jnp.arange(PER_SEQ * 8, dtype=jnp.int32)
    block_of_source = jnp.repeat(block_order, 8)
    slot_of_source = (block_of_source - sequence * PER_SEQ) * 8 + source % 8
    pick = (target[:, None] == slot_of_source[None, :]).astype(jnp.bfloat16)

    kv = jnp.concatenate(
        [keys.reshape(tok_rows, 4, HEAD_WIDTH), values.reshape(tok_rows, 4, HEAD_WIDTH)], axis=2
    )
    kv_got = scatter_rows(kv).reshape(1024, 2 * HEAD_WIDTH)
    kv_mine = jnp.dot(pick, kv_got, preferred_element_type=jnp.float32).astype(jnp.bfloat16)
    kv_all = lax.all_gather(kv_mine, "seq", axis=0, tiled=False)

    q_got = scatter_rows(queries.reshape(tok_rows, 4, HEADS * HEAD_WIDTH))
    q_got = q_got.reshape(1024, HEADS * HEAD_WIDTH)
    q_mine = jnp.dot(pick, q_got, preferred_element_type=jnp.float32).astype(jnp.bfloat16)

    out = attend(q_mine, kv_all, meta)

    back = lax.dot_general(
        pick, out, (((0,), (0,)), ((), ())), preferred_element_type=jnp.float32
    ).astype(jnp.bfloat16)
    home = lax.all_to_all(
        back.reshape(256, 4, HEADS * HEAD_WIDTH), ALL, split_axis=0, concat_axis=0, tiled=True
    )
    my_sequence = lax.dynamic_slice_in_dim(block_order, place // 2, 1, 0)[0] // PER_SEQ
    home = lax.dynamic_index_in_dim(
        home.reshape(2, MEMBERS, 4, 4, HEADS * HEAD_WIDTH), my_sequence, 0, keepdims=False
    )
    return home.transpose(0, 2, 1, 3).reshape(tok_rows, 4 * HEADS * HEAD_WIDTH)


def solution(mesh):
    rows = P(ALL, None)
    return jax.shard_map(
        body,
        mesh=mesh,
        in_specs=(rows, rows, rows, P(), P()),
        out_specs=rows,
        check_vma=False,
    )
```

```python
import math

import jax
import jax.numpy as jnp
from jax import lax
from jax.experimental import pallas as pl
from jax.experimental.pallas import tpu as pltpu
from jax.sharding import PartitionSpec as P

WIDTH = 128
ALL = ("dp", "seq", "head")
HEADS = 7
BLOCK = 256
HALF = 128
PER_SEQ = 64
BLOCKS = 128
SPREAD = 4
PART = HALF // SPREAD
ITEMS = 32
LANES = HEADS * PART
NOTES = 16
PIECE = LANES + NOTES
RUN = 64
KEYS = 2 * RUN
STEP = 2 * KEYS
UNITS = 8
TURNS = 72
PARTS = 9
NEG = -1e30
SCALE = math.log2(math.e) / math.sqrt(WIDTH)


def make_table(counts, pair_of, item_first, place_of, item_sequence):
    ends = jnp.cumsum(counts)
    total = ends[-1]
    turns = jnp.maximum((total + UNITS - 1) // UNITS, jnp.max(counts))
    slot = jnp.arange(TURNS * UNITS, dtype=jnp.int32)
    number = (slot % UNITS) * turns + slot // UNITS
    live = (slot // UNITS < turns) & (number < total)
    item = jnp.sum((number[:, None] >= ends[None, :]).astype(jnp.int32), axis=1)
    mine = (item[:, None] == jnp.arange(ITEMS, dtype=jnp.int32)[None, :]).astype(jnp.int32)

    def of_item(values):
        return jnp.sum(mine * values[None, :], axis=1)

    pair = pair_of(number - of_item(ends - counts), of_item)
    block = of_item(item_first) + 2 * pair
    index = of_item(item_sequence) * PER_SEQ + block
    options = jnp.arange(BLOCKS, dtype=jnp.int32)

    def find(at):
        hit = jnp.minimum(at, BLOCKS - 1)[:, None] == options[None, :]
        return jnp.sum(hit.astype(jnp.int32) * place_of[None, :], axis=1)

    packed = item + (find(index) << 6) + (find(index + 1) << 13) + (block << 20)
    return jnp.where(live, packed, ITEMS), turns


def plan(doc_lengths, block_order, dp, plane):
    order = block_order.astype(jnp.int32)
    block = jnp.arange(BLOCKS, dtype=jnp.int32)
    place = ((block // 64) * 2 + block % 2) * 32 + (block // 2) % 32
    place_of = jnp.sum(
        (order[None, :] == block[:, None]).astype(jnp.int32) * place[None, :], axis=1
    )
    held = 2 * (dp * 32 + jnp.arange(ITEMS, dtype=jnp.int32)) + plane // 2
    chosen = (held[:, None] == block[None, :]).astype(jnp.int32)
    number = jnp.sum(chosen * order[None, :], axis=1)
    sequence, index = number // PER_SEQ, number % PER_SEQ
    ends = jnp.cumsum(doc_lengths.astype(jnp.int32), axis=1)[:, :2]
    first_end = jnp.where(sequence == 0, ends[0, 0], ends[1, 0])
    second_end = jnp.where(sequence == 0, ends[0, 1], ends[1, 1])

    def start_of(position):
        return jnp.where(
            position >= second_end, second_end, jnp.where(position >= first_end, first_end, 0)
        )

    low = index * BLOCK + (plane % 2) * HALF
    first = start_of(low) // BLOCK
    clean = (start_of(low + HALF - 1) + BLOCK - 1) // BLOCK
    pairs = (index - first) // 2 + 1
    edge = jnp.clip((clean - first + 1) // 2, 0, pairs)
    masked = edge + (edge < pairs).astype(jnp.int32)
    free = pairs - masked

    def masked_pair(at, of_item):
        return jnp.where(at < of_item(edge), at, of_item(pairs) - 1)

    def free_pair(at, of_item):
        return at + of_item(edge)

    table_m, turns_m = make_table(masked, masked_pair, first, place_of, sequence)
    table_f, turns_f = make_table(free, free_pair, first, place_of, sequence)
    spots = jnp.concatenate([low, jnp.zeros((1,), jnp.int32)])
    starts = jnp.concatenate([first_end, second_end])
    return table_m, table_f, spots, starts, jnp.stack([turns_m, turns_f])


def attend_kernel(
    table_m, table_f, spots, starts, meta, q_ref, *refs
):
    parts, (o_ref, kv_ref, arrived, held, tops, peak, total, sums) = refs[:PARTS], refs[PARTS:]
    half, part, plane, core = meta[2], meta[3], meta[4], meta[5]

    copies = []

    def bring(source, target):
        copies.append(pltpu.make_async_copy(source, target, arrived.at[len(copies)]))
        copies[-1].start()

    bring(parts[0], kv_ref.at[plane])
    for step in range(1, 4):
        behind, ahead = (plane + 8 - step) % 8, (plane + step) % 8
        bring(parts[2 * step - 1], kv_ref.at[jnp.where(core == 0, behind, ahead)])
        bring(parts[2 * step], kv_ref.at[jnp.where(core == 0, ahead, behind)])
    across = (plane + 4) % 8
    bring(parts[7], kv_ref.at[across, pl.ds(core * 16, 16)])
    bring(parts[8], kv_ref.at[across, pl.ds((1 - core) * 16, 16)])
    peak[...] = jnp.full(peak.shape, NEG, jnp.float32)
    total[...] = jnp.zeros(total.shape, jnp.float32)
    sums[...] = jnp.zeros(sums.shape, jnp.float32)
    q_places = lax.broadcasted_iota(jnp.int32, (1, LANES), 1) % PART + part * PART
    key = lax.broadcasted_iota(jnp.int32, (STEP, 1), 0)
    k_places = (key // KEYS) * BLOCK + ((key % KEYS) // RUN) * HALF + half * RUN + key % RUN

    for copy in copies:
        copy.wait()

    def fetch(word, columns):
        pieces = []
        for place in ((word >> 6) & 127, (word >> 13) & 127):
            first, at = (place >> 5) * 2, place & 31
            pieces += [kv_ref[first, at, :, columns], kv_ref[first + 1, at, :, columns]]
        return jnp.concatenate(pieces, axis=0)

    def score(table, at, masked, slot):
        for s in range(UNITS):
            word = table[at * UNITS + s]
            item = word & 63
            known = jnp.minimum(item, ITEMS - 1)
            value = SCALE * lax.dot_general(
                fetch(word, slice(0, WIDTH)),
                q_ref[known],
                (((1,), (1,)), ((), ())),
                preferred_element_type=jnp.float32,
            )
            if masked:
                q_spots = q_places + spots[item]
                one_end, two_end = starts[known], starts[ITEMS + known]
                begin = jnp.where(
                    q_spots >= two_end, two_end, jnp.where(q_spots >= one_end, one_end, 0)
                )
                k_spots = k_places + (word >> 20) * BLOCK
                value = jnp.where((k_spots <= q_spots) & (k_spots >= begin), value, NEG)
            held[slot, s] = value
            tops[slot, s] = jnp.max(value.reshape(STEP // 8, 8, LANES), axis=0)

    def absorb(table, at, slot):
        words = [table[at * UNITS + s] for s in range(UNITS)]
        items = [word & 63 for word in words]
        before = [peak[item] for item in items]
        now = []
        for s, old in enumerate(before):
            now.append(jnp.maximum(old, jnp.max(tops[slot, s], axis=0, keepdims=True)))
        fades = [jnp.exp2(old - new) for old, new in zip(before, now)]
        for item, new in zip(items, now):
            peak[item] = new
        added, updates = [], []
        for s, (word, new) in enumerate(zip(words, now)):
            weight = jnp.exp2(held[slot, s].reshape(STEP // 8, 8, LANES) - new[None])
            added.append(jnp.sum(weight, axis=0))
            updates.append(
                lax.dot_general(
                    fetch(word, slice(WIDTH, 2 * WIDTH)),
                    weight.reshape(STEP, LANES).astype(jnp.bfloat16),
                    (((0,), (0,)), ((), ())),
                    preferred_element_type=jnp.float32,
                )
            )
        totals = [total[item] for item in items]
        for item, old, fade, more in zip(items, totals, fades, added):
            total[item] = old * fade + more
        for item, fade, update in zip(items, fades, updates):
            kept = sums[item].reshape(WIDTH // 8, 8, LANES) * fade[None]
            sums[item] = kept.reshape(WIDTH, LANES) + update

    def run(table, turns, masked):
        score(table, 0, masked, 0)

        @pl.loop(0, (turns + 1) // 2)
        def _(pair):
            score(table, 2 * pair + 1, masked, 1)
            absorb(table, 2 * pair, 0)
            score(table, 2 * pair + 2, masked, 0)
            absorb(table, 2 * pair + 1, 1)

    run(table_m, meta[0], True)
    run(table_f, meta[1], False)

    sublane = lax.broadcasted_iota(jnp.int32, (8, WIDTH), 0)
    filler = jnp.zeros((8, 2 * WIDTH - LANES), jnp.float32)

    def finish(item):
        whole = jnp.sum(total[item], axis=0, keepdims=True)
        mean = sums[item] * (1.0 / whole)
        level = peak[item] + jnp.log2(whole)
        high = level.astype(jnp.bfloat16).astype(jnp.float32)
        middle = (level - high).astype(jnp.bfloat16).astype(jnp.float32)
        low = level - high - middle
        notes = jnp.zeros((8, WIDTH), jnp.float32)
        for at, piece in enumerate((high, middle, low)):
            left, right = piece[:, :WIDTH], jnp.concatenate([piece[:, WIDTH:], filler], axis=1)
            notes = jnp.where(sublane == 2 * at, left, notes)
            notes = jnp.where(sublane == 2 * at + 1, right, notes)
        block = jnp.concatenate([mean.T, notes, jnp.zeros_like(notes)], axis=0)
        o_ref[item] = block.astype(jnp.bfloat16)

    @pl.loop(0, ITEMS // 4)
    def _(at):
        for more in range(4):
            finish(at * 4 + more)


def attend(queries, keys_values, tables, half, part, plane, core):
    table_m, table_f, spots, starts, turns = tables
    meta = jnp.concatenate([turns, jnp.stack([half, part, plane, core])]).astype(jnp.int32)
    once = pl.Buffered(1)
    return pl.pallas_call(
        attend_kernel,
        out_shape=jax.ShapeDtypeStruct((ITEMS, PIECE, WIDTH), jnp.bfloat16),
        grid_spec=pltpu.PrefetchScalarGridSpec(
            num_scalar_prefetch=5,
            grid=(1,),
            in_specs=[
                pl.BlockSpec(queries.shape, lambda i, *_: (0, 0, 0), pipeline_mode=once),
            ]
            + [pl.BlockSpec(memory_space=pl.ANY)] * PARTS,
            out_specs=pl.BlockSpec((ITEMS, PIECE, WIDTH), lambda i, *_: (0, 0, 0)),
            scratch_shapes=[
                pltpu.VMEM((8, 32, RUN, 2 * WIDTH), jnp.bfloat16),
                pltpu.SemaphoreType.DMA((PARTS,)),
                pltpu.VMEM((2, UNITS, STEP, LANES), jnp.float32),
                pltpu.VMEM((2, UNITS, 8, LANES), jnp.float32),
                pltpu.VMEM((ITEMS + 1, 8, LANES), jnp.float32),
                pltpu.VMEM((ITEMS + 1, 8, LANES), jnp.float32),
                pltpu.VMEM((ITEMS + 1, WIDTH, LANES), jnp.float32),
            ],
        ),
        compiler_params=pltpu.CompilerParams(vmem_limit_bytes=48 * 1024 * 1024),
    )(table_m, table_f, spots, starts, meta, queries, *keys_values)


def join_kernel(got_ref, out_ref):
    for part in range(SPREAD):
        one = got_ref[0, 0, part].astype(jnp.float32)
        two = got_ref[0, 1, part].astype(jnp.float32)
        levels = [x[LANES : LANES + 2] + x[LANES + 2 : LANES + 4] + x[LANES + 4 : LANES + 6] for x in (one, two)]
        ahead = levels[1] - levels[0]
        shares = jnp.concatenate(
            [1.0 / (1.0 + jnp.exp2(ahead)), 1.0 / (1.0 + jnp.exp2(-ahead))], axis=0
        )
        shares = jnp.concatenate([shares, shares], axis=0).T
        for head in range(HEADS):
            rows = slice(head * PART, (head + 1) * PART)
            at, column = head * PART % WIDTH, head * PART // WIDTH
            joined = one[rows] * shares[at : at + PART, column : column + 1]
            joined = joined + two[rows] * shares[at : at + PART, column + 2 : column + 3]
            out_ref[part * PART : (part + 1) * PART, head * WIDTH : (head + 1) * WIDTH] = (
                joined.astype(jnp.bfloat16)
            )


def join(got):
    return pl.pallas_call(
        join_kernel,
        out_shape=jax.ShapeDtypeStruct((HALF, 4 * HEADS * WIDTH), jnp.bfloat16),
        grid=(4,),
        in_specs=[pl.BlockSpec((1,) + got.shape[1:], lambda i: (i, 0, 0, 0, 0))],
        out_specs=pl.BlockSpec((HALF, HEADS * WIDTH), lambda i: (0, i)),
        compiler_params=pltpu.CompilerParams(vmem_limit_bytes=24 * 1024 * 1024),
    )(got)


def gather_planes(kv, core):
    def device(member, plane):
        return ((plane // 4) * 32 + member) * 4 + plane % 4

    every = [(member, plane) for member in range(32) for plane in range(8)]
    onward = [(device(m, z), device(m, (z + 1 - 2 * (m % 2)) % 8)) for m, z in every]
    swap = [(device(m, z), device(m ^ 1, z)) for m, z in every]
    parts, passing = [kv], kv
    for _ in range(3):
        passing = lax.ppermute(passing, ALL, onward)
        parts += [passing, lax.ppermute(passing, ALL, swap)]
    last = lax.ppermute(lax.dynamic_slice_in_dim(passing, core * 16, 16, 0), ALL, onward)
    return parts + [last, lax.ppermute(last, ALL, swap)]


def body(queries, keys, values, doc_lengths, block_order):
    member = lax.axis_index("seq")
    half, part, core = (member // SPREAD) % 2, member % SPREAD, member % 2
    plane = lax.axis_index("dp") * 4 + lax.axis_index("head")

    kv = jnp.concatenate(
        [keys.reshape(2, RUN, 4, WIDTH), values.reshape(2, RUN, 4, WIDTH)], axis=3
    )
    kv = jnp.broadcast_to(kv.transpose(2, 0, 1, 3)[:, :, None], (4, 2, SPREAD, RUN, 2 * WIDTH))
    kv = kv.reshape(32, RUN, 2 * WIDTH)
    kv = lax.all_to_all(kv, "seq", split_axis=0, concat_axis=0, tiled=True)
    keys_values = gather_planes(kv, core)

    pieces = queries.reshape(SPREAD, PART, 4, HEADS, WIDTH).transpose(2, 0, 3, 1, 4)
    pieces = jnp.broadcast_to(pieces[:, None], (4, 2) + pieces.shape[1:])
    pieces = pieces.reshape(32, LANES, WIDTH)
    got = lax.all_to_all(pieces, "seq", split_axis=0, concat_axis=0, tiled=True)

    tables = plan(doc_lengths, block_order, lax.axis_index("dp"), lax.axis_index("head"))
    out = attend(got, keys_values, tables, half, part, plane, core)
    home = lax.all_to_all(out, "seq", split_axis=0, concat_axis=0, tiled=True)
    return join(home.reshape(4, 2, SPREAD, PIECE, WIDTH))


def solution(mesh):
    rows = P(ALL, None)
    return jax.shard_map(
        body,
        mesh=mesh,
        in_specs=(rows, rows, rows, P(), P()),
        out_specs=rows,
        check_vma=False,
    )
```

```python
import math

import jax
import jax.numpy as jnp
from jax import lax
from jax.experimental import pallas as pl
from jax.experimental.pallas import tpu as pltpu
from jax.sharding import PartitionSpec as P

WIDTH = 128
ALL = ("dp", "seq", "head")
HEADS = 7
BLOCK = 256
HALF = 128
PER_SEQ = 64
BLOCKS = 128
SPREAD = 4
PART = HALF // SPREAD
ITEMS = 32
LANES = HEADS * PART
NOTES = 16
PIECE = LANES + NOTES
RUN = 64
KEYS = 2 * RUN
STEP = 2 * KEYS
UNITS = 8
TURNS = 72
PARTS = 9
NEG = -1e30
SCALE = math.log2(math.e) / math.sqrt(WIDTH)


def make_table(counts, pair_of, item_first, place_of, item_sequence):
    ends = jnp.cumsum(counts)
    total = ends[-1]
    turns = jnp.maximum((total + UNITS - 1) // UNITS, jnp.max(counts))
    slot = jnp.arange(TURNS * UNITS, dtype=jnp.int32)
    number = (slot % UNITS) * turns + slot // UNITS
    live = (slot // UNITS < turns) & (number < total)
    item = jnp.sum((number[:, None] >= ends[None, :]).astype(jnp.int32), axis=1)
    mine = (item[:, None] == jnp.arange(ITEMS, dtype=jnp.int32)[None, :]).astype(jnp.int32)

    def of_item(values):
        return jnp.sum(mine * values[None, :], axis=1)

    pair = pair_of(number - of_item(ends - counts), of_item)
    block = of_item(item_first) + 2 * pair
    index = of_item(item_sequence) * PER_SEQ + block
    options = jnp.arange(BLOCKS, dtype=jnp.int32)

    def find(at):
        hit = jnp.minimum(at, BLOCKS - 1)[:, None] == options[None, :]
        return jnp.sum(hit.astype(jnp.int32) * place_of[None, :], axis=1)

    packed = item + (find(index) << 6) + (find(index + 1) << 13) + (block << 20)
    return jnp.where(live, packed, ITEMS), turns


def plan(doc_lengths, block_order, dp, plane):
    order = block_order.astype(jnp.int32)
    block = jnp.arange(BLOCKS, dtype=jnp.int32)
    place = ((block // 64) * 2 + block % 2) * 32 + (block // 2) % 32
    place_of = jnp.sum(
        (order[None, :] == block[:, None]).astype(jnp.int32) * place[None, :], axis=1
    )
    held = 2 * (dp * 32 + jnp.arange(ITEMS, dtype=jnp.int32)) + plane // 2
    chosen = (held[:, None] == block[None, :]).astype(jnp.int32)
    number = jnp.sum(chosen * order[None, :], axis=1)
    sequence, index = number // PER_SEQ, number % PER_SEQ
    ends = jnp.cumsum(doc_lengths.astype(jnp.int32), axis=1)[:, :2]
    first_end = jnp.where(sequence == 0, ends[0, 0], ends[1, 0])
    second_end = jnp.where(sequence == 0, ends[0, 1], ends[1, 1])

    def start_of(position):
        return jnp.where(
            position >= second_end, second_end, jnp.where(position >= first_end, first_end, 0)
        )

    low = index * BLOCK + (plane % 2) * HALF
    first = start_of(low) // BLOCK
    clean = (start_of(low + HALF - 1) + BLOCK - 1) // BLOCK
    pairs = (index - first) // 2 + 1
    edge = jnp.clip((clean - first + 1) // 2, 0, pairs)
    masked = edge + (edge < pairs).astype(jnp.int32)
    free = pairs - masked
    turns = jnp.maximum((jnp.sum(masked) + UNITS - 1) // UNITS, jnp.max(masked))
    room = turns * UNITS - jnp.sum(masked)
    levels = jnp.arange(PER_SEQ // 2 + 1, dtype=jnp.int32)
    moved = jnp.minimum(
        jnp.maximum(free[None, :] - levels[:, None], 0), (turns - masked)[None, :]
    )
    fits = jnp.sum(moved, axis=1) <= room
    level = jnp.min(jnp.where(fits, levels, PER_SEQ // 2))
    more = jnp.minimum(jnp.maximum(free - level, 0), turns - masked)
    edge, masked, free = edge + more, masked + more, free - more

    def masked_pair(at, of_item):
        return jnp.where(at < of_item(edge), at, of_item(pairs) - 1)

    def free_pair(at, of_item):
        return at + of_item(edge)

    table_m, turns_m = make_table(masked, masked_pair, first, place_of, sequence)
    table_f, turns_f = make_table(free, free_pair, first, place_of, sequence)
    spots = jnp.concatenate([low, jnp.zeros((1,), jnp.int32)])
    starts = jnp.concatenate([first_end, second_end])
    return table_m, table_f, spots, starts, jnp.stack([turns_m, turns_f])


def attend_kernel(
    table_m, table_f, spots, starts, meta, q_ref, *refs
):
    parts, (o_ref, kv_ref, arrived, held, tops, peak, total, sums) = refs[:PARTS], refs[PARTS:]
    half, part, plane, core = meta[2], meta[3], meta[4], meta[5]

    copies = []

    def bring(source, target):
        copies.append(pltpu.make_async_copy(source, target, arrived.at[len(copies)]))
        copies[-1].start()

    bring(parts[0], kv_ref.at[plane])
    for step in range(1, 4):
        behind, ahead = (plane + 8 - step) % 8, (plane + step) % 8
        bring(parts[2 * step - 1], kv_ref.at[jnp.where(core == 0, behind, ahead)])
        bring(parts[2 * step], kv_ref.at[jnp.where(core == 0, ahead, behind)])
    across = (plane + 4) % 8
    bring(parts[7], kv_ref.at[across, pl.ds(core * 16, 16)])
    bring(parts[8], kv_ref.at[across, pl.ds((1 - core) * 16, 16)])
    peak[...] = jnp.full(peak.shape, NEG, jnp.float32)
    total[...] = jnp.zeros(total.shape, jnp.float32)
    sums[...] = jnp.zeros(sums.shape, jnp.float32)
    q_places = lax.broadcasted_iota(jnp.int32, (1, LANES), 1) % PART + part * PART
    key = lax.broadcasted_iota(jnp.int32, (STEP, 1), 0)
    k_places = (key // KEYS) * BLOCK + ((key % KEYS) // RUN) * HALF + half * RUN + key % RUN

    for copy in copies:
        copy.wait()

    def fetch(word, columns):
        pieces = []
        for place in ((word >> 6) & 127, (word >> 13) & 127):
            first, at = (place >> 5) * 2, place & 31
            pieces += [kv_ref[first, at, :, columns], kv_ref[first + 1, at, :, columns]]
        return jnp.concatenate(pieces, axis=0)

    def score(table, at, masked, slot):
        for s in range(UNITS):
            word = table[at * UNITS + s]
            item = word & 63
            known = jnp.minimum(item, ITEMS - 1)
            value = SCALE * lax.dot_general(
                fetch(word, slice(0, WIDTH)),
                q_ref[known],
                (((1,), (1,)), ((), ())),
                preferred_element_type=jnp.float32,
            )
            if masked:
                q_spots = q_places + spots[item]
                one_end, two_end = starts[known], starts[ITEMS + known]
                begin = jnp.where(
                    q_spots >= two_end, two_end, jnp.where(q_spots >= one_end, one_end, 0)
                )
                k_spots = k_places + (word >> 20) * BLOCK
                value = jnp.where((k_spots <= q_spots) & (k_spots >= begin), value, NEG)
            held[slot, s] = value
            tops[slot, s] = jnp.max(value.reshape(STEP // 8, 8, LANES), axis=0)

    def absorb(table, at, slot):
        words = [table[at * UNITS + s] for s in range(UNITS)]
        items = [word & 63 for word in words]
        before = [peak[item] for item in items]
        now = []
        for s, old in enumerate(before):
            now.append(jnp.maximum(old, jnp.max(tops[slot, s], axis=0, keepdims=True)))
        fades = [jnp.exp2(old - new) for old, new in zip(before, now)]
        for item, new in zip(items, now):
            peak[item] = new
        added, updates = [], []
        for s, (word, new) in enumerate(zip(words, now)):
            weight = jnp.exp2(held[slot, s].reshape(STEP // 8, 8, LANES) - new[None])
            added.append(jnp.sum(weight, axis=0))
            updates.append(
                lax.dot_general(
                    fetch(word, slice(WIDTH, 2 * WIDTH)),
                    weight.reshape(STEP, LANES).astype(jnp.bfloat16),
                    (((0,), (0,)), ((), ())),
                    preferred_element_type=jnp.float32,
                )
            )
        totals = [total[item] for item in items]
        for item, old, fade, more in zip(items, totals, fades, added):
            total[item] = old * fade + more
        for item, fade, update in zip(items, fades, updates):
            kept = sums[item].reshape(WIDTH // 8, 8, LANES) * fade[None]
            sums[item] = kept.reshape(WIDTH, LANES) + update

    def run(table, turns, masked):
        score(table, 0, masked, 0)

        @pl.loop(0, (turns + 1) // 2)
        def _(pair):
            score(table, 2 * pair + 1, masked, 1)
            absorb(table, 2 * pair, 0)
            score(table, 2 * pair + 2, masked, 0)
            absorb(table, 2 * pair + 1, 1)

    run(table_m, meta[0], True)
    run(table_f, meta[1], False)

    sublane = lax.broadcasted_iota(jnp.int32, (8, WIDTH), 0)
    filler = jnp.zeros((8, 2 * WIDTH - LANES), jnp.float32)

    def finish(item):
        whole = jnp.sum(total[item], axis=0, keepdims=True)
        mean = sums[item] * (1.0 / whole)
        level = peak[item] + jnp.log2(whole)
        high = level.astype(jnp.bfloat16).astype(jnp.float32)
        middle = (level - high).astype(jnp.bfloat16).astype(jnp.float32)
        low = level - high - middle
        notes = jnp.zeros((8, WIDTH), jnp.float32)
        for at, piece in enumerate((high, middle, low)):
            left, right = piece[:, :WIDTH], jnp.concatenate([piece[:, WIDTH:], filler], axis=1)
            notes = jnp.where(sublane == 2 * at, left, notes)
            notes = jnp.where(sublane == 2 * at + 1, right, notes)
        block = jnp.concatenate([mean.T, notes, jnp.zeros_like(notes)], axis=0)
        o_ref[item] = block.astype(jnp.bfloat16)

    @pl.loop(0, ITEMS // 4)
    def _(at):
        for more in range(4):
            finish(at * 4 + more)


def attend(queries, keys_values, tables, half, part, plane, core):
    table_m, table_f, spots, starts, turns = tables
    meta = jnp.concatenate([turns, jnp.stack([half, part, plane, core])]).astype(jnp.int32)
    once = pl.Buffered(1)
    return pl.pallas_call(
        attend_kernel,
        out_shape=jax.ShapeDtypeStruct((ITEMS, PIECE, WIDTH), jnp.bfloat16),
        grid_spec=pltpu.PrefetchScalarGridSpec(
            num_scalar_prefetch=5,
            grid=(1,),
            in_specs=[
                pl.BlockSpec(queries.shape, lambda i, *_: (0, 0, 0), pipeline_mode=once),
            ]
            + [pl.BlockSpec(memory_space=pl.ANY)] * PARTS,
            out_specs=pl.BlockSpec((ITEMS, PIECE, WIDTH), lambda i, *_: (0, 0, 0)),
            scratch_shapes=[
                pltpu.VMEM((8, 32, RUN, 2 * WIDTH), jnp.bfloat16),
                pltpu.SemaphoreType.DMA((PARTS,)),
                pltpu.VMEM((2, UNITS, STEP, LANES), jnp.float32),
                pltpu.VMEM((2, UNITS, 8, LANES), jnp.float32),
                pltpu.VMEM((ITEMS + 1, 8, LANES), jnp.float32),
                pltpu.VMEM((ITEMS + 1, 8, LANES), jnp.float32),
                pltpu.VMEM((ITEMS + 1, WIDTH, LANES), jnp.float32),
            ],
        ),
        compiler_params=pltpu.CompilerParams(vmem_limit_bytes=48 * 1024 * 1024),
    )(table_m, table_f, spots, starts, meta, queries, *keys_values)


def join_kernel(got_ref, out_ref):
    for part in range(SPREAD):
        one = got_ref[0, 0, part].astype(jnp.float32)
        two = got_ref[0, 1, part].astype(jnp.float32)
        levels = [
            x[LANES : LANES + 2] + x[LANES + 2 : LANES + 4] + x[LANES + 4 : LANES + 6]
            for x in (one, two)
        ]
        ahead = levels[1] - levels[0]
        shares = jnp.concatenate(
            [1.0 / (1.0 + jnp.exp2(ahead)), 1.0 / (1.0 + jnp.exp2(-ahead))], axis=0
        )
        shares = jnp.concatenate([shares, shares], axis=0).T
        for head in range(HEADS):
            rows = slice(head * PART, (head + 1) * PART)
            at, column = head * PART % WIDTH, head * PART // WIDTH
            joined = one[rows] * shares[at : at + PART, column : column + 1]
            joined = joined + two[rows] * shares[at : at + PART, column + 2 : column + 3]
            out_ref[part * PART : (part + 1) * PART, head * WIDTH : (head + 1) * WIDTH] = (
                joined.astype(jnp.bfloat16)
            )


def join(got):
    return pl.pallas_call(
        join_kernel,
        out_shape=jax.ShapeDtypeStruct((HALF, 4 * HEADS * WIDTH), jnp.bfloat16),
        grid=(4,),
        in_specs=[pl.BlockSpec((1,) + got.shape[1:], lambda i: (i, 0, 0, 0, 0))],
        out_specs=pl.BlockSpec((HALF, HEADS * WIDTH), lambda i: (0, i)),
        compiler_params=pltpu.CompilerParams(vmem_limit_bytes=24 * 1024 * 1024),
    )(got)


def pack_queries_kernel(q_ref, out_ref):
    for part in range(SPREAD):
        for head in range(HEADS):
            block = q_ref[part * PART : (part + 1) * PART, head * WIDTH : (head + 1) * WIDTH]
            for half in range(2):
                out_ref[0, half, part, head * PART : (head + 1) * PART, :] = block


def pack_queries(queries):
    packed = pl.pallas_call(
        pack_queries_kernel,
        out_shape=jax.ShapeDtypeStruct((4, 2, SPREAD, LANES, WIDTH), queries.dtype),
        grid=(4,),
        in_specs=[pl.BlockSpec((HALF, HEADS * WIDTH), lambda i: (0, i))],
        out_specs=pl.BlockSpec((1, 2, SPREAD, LANES, WIDTH), lambda i: (i, 0, 0, 0, 0)),
    )(queries)
    return packed.reshape(32, LANES, WIDTH)


def pack_keys_kernel(k_ref, v_ref, out_ref):
    for head in range(4):
        columns = slice(head * WIDTH, (head + 1) * WIDTH)
        for half in range(2):
            rows = slice(half * RUN, (half + 1) * RUN)
            for part in range(SPREAD):
                out_ref[head, half, part, :, :WIDTH] = k_ref[rows, columns]
                out_ref[head, half, part, :, WIDTH:] = v_ref[rows, columns]


def pack_keys(keys, values):
    packed = pl.pallas_call(
        pack_keys_kernel,
        out_shape=jax.ShapeDtypeStruct((4, 2, SPREAD, RUN, 2 * WIDTH), keys.dtype),
    )(keys, values)
    return packed.reshape(32, RUN, 2 * WIDTH)


def gather_planes(kv, core, tables, pieces):
    def device(member, plane):
        return ((plane // 4) * 32 + member) * 4 + plane % 4

    every = [(member, plane) for member in range(32) for plane in range(8)]
    onward = [(device(m, z), device(m, (z + 1 - 2 * (m % 2)) % 8)) for m, z in every]
    swap = [(device(m, z), device(m ^ 1, z)) for m, z in every]
    first = lax.ppermute(kv, ALL, onward)
    first, tables, pieces = lax.optimization_barrier((first, tables, pieces))
    second = lax.ppermute(first, ALL, onward)
    first_swapped = lax.ppermute(first, ALL, swap)
    third = lax.ppermute(second, ALL, onward)
    second_swapped = lax.ppermute(second, ALL, swap)
    last = lax.ppermute(lax.dynamic_slice_in_dim(third, core * 16, 16, 0), ALL, onward)
    third_swapped = lax.ppermute(third, ALL, swap)
    last_swapped = lax.ppermute(last, ALL, swap)
    parts = [kv, first, first_swapped, second, second_swapped]
    return parts + [third, third_swapped, last, last_swapped], tables, pieces


def body(queries, keys, values, doc_lengths, block_order):
    member = lax.axis_index("seq")
    half, part, core = (member // SPREAD) % 2, member % SPREAD, member % 2
    plane = lax.axis_index("dp") * 4 + lax.axis_index("head")

    kv = lax.all_to_all(
        pack_keys(keys, values), "seq", split_axis=0, concat_axis=0, tiled=True
    )
    tables = plan(doc_lengths, block_order, lax.axis_index("dp"), lax.axis_index("head"))
    keys_values, tables, pieces = gather_planes(kv, core, tables, pack_queries(queries))
    got = lax.all_to_all(pieces, "seq", split_axis=0, concat_axis=0, tiled=True)
    out = attend(got, keys_values, tables, half, part, plane, core)
    home = lax.all_to_all(out, "seq", split_axis=0, concat_axis=0, tiled=True)
    return join(home.reshape(4, 2, SPREAD, PIECE, WIDTH))


def solution(mesh):
    rows = P(ALL, None)
    return jax.shard_map(
        body,
        mesh=mesh,
        in_specs=(rows, rows, rows, P(), P()),
        out_specs=rows,
        check_vma=False,
    )
```

```python
import math

import jax
import jax.numpy as jnp
from jax import lax
from jax.experimental import pallas as pl
from jax.experimental.pallas import tpu as pltpu
from jax.sharding import PartitionSpec as P

WIDTH = 128
ALL = ("dp", "seq", "head")
HEADS = 7
BLOCK = 256
HALF = 128
PER_SEQ = 64
BLOCKS = 128
SPREAD = 4
PART = HALF // SPREAD
ITEMS = 32
LANES = HEADS * PART
NOTES = 16
PIECE = LANES + NOTES
RUN = 64
KEYS = 2 * RUN
STEP = 2 * KEYS
UNITS = 8
TURNS = 72
PARTS = 9
NEG = -1e30
SCALE = math.log2(math.e) / math.sqrt(WIDTH)


def make_table(counts, pair_of, item_first, place_of, item_sequence):
    ends = jnp.cumsum(counts)
    total = ends[-1]
    turns = jnp.maximum((total + UNITS - 1) // UNITS, jnp.max(counts))
    slot = jnp.arange(TURNS * UNITS, dtype=jnp.int32)
    number = (slot % UNITS) * turns + slot // UNITS
    live = (slot // UNITS < turns) & (number < total)
    item = jnp.sum((number[:, None] >= ends[None, :]).astype(jnp.int32), axis=1)
    mine = (item[:, None] == jnp.arange(ITEMS, dtype=jnp.int32)[None, :]).astype(jnp.int32)

    def of_item(values):
        return jnp.sum(mine * values[None, :], axis=1)

    pair = pair_of(number - of_item(ends - counts), of_item)
    block = of_item(item_first) + 2 * pair
    index = of_item(item_sequence) * PER_SEQ + block
    options = jnp.arange(BLOCKS, dtype=jnp.int32)

    def find(at):
        hit = jnp.minimum(at, BLOCKS - 1)[:, None] == options[None, :]
        return jnp.sum(hit.astype(jnp.int32) * place_of[None, :], axis=1)

    packed = item + (find(index) << 6) + (find(index + 1) << 13) + (block << 20)
    return jnp.where(live, packed, ITEMS), turns


def plan(doc_lengths, block_order, dp, plane):
    order = block_order.astype(jnp.int32)
    block = jnp.arange(BLOCKS, dtype=jnp.int32)
    place = ((block // 64) * 2 + block % 2) * 32 + (block // 2) % 32
    place_of = jnp.sum(
        (order[None, :] == block[:, None]).astype(jnp.int32) * place[None, :], axis=1
    )
    held = 2 * (dp * 32 + jnp.arange(ITEMS, dtype=jnp.int32)) + plane // 2
    chosen = (held[:, None] == block[None, :]).astype(jnp.int32)
    number = jnp.sum(chosen * order[None, :], axis=1)
    sequence, index = number // PER_SEQ, number % PER_SEQ
    ends = jnp.cumsum(doc_lengths.astype(jnp.int32), axis=1)[:, :2]
    first_end = jnp.where(sequence == 0, ends[0, 0], ends[1, 0])
    second_end = jnp.where(sequence == 0, ends[0, 1], ends[1, 1])

    def start_of(position):
        return jnp.where(
            position >= second_end, second_end, jnp.where(position >= first_end, first_end, 0)
        )

    low = index * BLOCK + (plane % 2) * HALF
    first = start_of(low) // BLOCK
    clean = (start_of(low + HALF - 1) + BLOCK - 1) // BLOCK
    pairs = (index - first) // 2 + 1
    edge = jnp.clip((clean - first + 1) // 2, 0, pairs)
    masked = edge + (edge < pairs).astype(jnp.int32)
    free = pairs - masked
    turns = jnp.maximum((jnp.sum(masked) + UNITS - 1) // UNITS, jnp.max(masked))
    room = turns * UNITS - jnp.sum(masked)
    levels = jnp.arange(PER_SEQ // 2 + 1, dtype=jnp.int32)
    moved = jnp.minimum(
        jnp.maximum(free[None, :] - levels[:, None], 0), (turns - masked)[None, :]
    )
    fits = jnp.sum(moved, axis=1) <= room
    level = jnp.min(jnp.where(fits, levels, PER_SEQ // 2))
    more = jnp.minimum(jnp.maximum(free - level, 0), turns - masked)
    edge, masked, free = edge + more, masked + more, free - more

    def masked_pair(at, of_item):
        return jnp.where(at < of_item(edge), at, of_item(pairs) - 1)

    def free_pair(at, of_item):
        return at + of_item(edge)

    table_m, turns_m = make_table(masked, masked_pair, first, place_of, sequence)
    table_f, turns_f = make_table(free, free_pair, first, place_of, sequence)
    spots = jnp.concatenate([low, jnp.zeros((1,), jnp.int32)])
    starts = jnp.concatenate([first_end, second_end])
    return table_m, table_f, spots, starts, jnp.stack([turns_m, turns_f])


def attend_kernel(
    table_m, table_f, spots, starts, meta, q_ref, *refs
):
    parts, (o_ref, kv_ref, arrived, held, tops, peak, total, sums) = refs[:PARTS], refs[PARTS:]
    half, part, plane, core = meta[2], meta[3], meta[4], meta[5]

    copies = []

    def bring(source, target):
        copies.append(pltpu.make_async_copy(source, target, arrived.at[len(copies)]))
        copies[-1].start()

    bring(parts[0], kv_ref.at[plane])
    for step in range(1, 4):
        behind, ahead = (plane + 8 - step) % 8, (plane + step) % 8
        bring(parts[2 * step - 1], kv_ref.at[jnp.where(core == 0, behind, ahead)])
        bring(parts[2 * step], kv_ref.at[jnp.where(core == 0, ahead, behind)])
    across = (plane + 4) % 8
    bring(parts[7], kv_ref.at[across, pl.ds(core * 16, 16)])
    bring(parts[8], kv_ref.at[across, pl.ds((1 - core) * 16, 16)])
    peak[...] = jnp.full(peak.shape, NEG, jnp.float32)
    total[...] = jnp.zeros(total.shape, jnp.float32)
    sums[...] = jnp.zeros(sums.shape, jnp.float32)
    q_places = lax.broadcasted_iota(jnp.int32, (1, LANES), 1) % PART + part * PART
    key = lax.broadcasted_iota(jnp.int32, (STEP, 1), 0)
    k_places = (key // KEYS) * BLOCK + ((key % KEYS) // RUN) * HALF + half * RUN + key % RUN

    for copy in copies:
        copy.wait()

    def fetch(word, columns):
        pieces = []
        for place in ((word >> 6) & 127, (word >> 13) & 127):
            first, at = (place >> 5) * 2, place & 31
            pieces += [kv_ref[first, at, :, columns], kv_ref[first + 1, at, :, columns]]
        return jnp.concatenate(pieces, axis=0)

    def score(table, at, masked, slot):
        for s in range(UNITS):
            word = table[at * UNITS + s]
            item = word & 63
            known = jnp.minimum(item, ITEMS - 1)
            value = SCALE * lax.dot_general(
                fetch(word, slice(0, WIDTH)),
                q_ref[known],
                (((1,), (1,)), ((), ())),
                preferred_element_type=jnp.float32,
            )
            if masked:
                q_spots = q_places + spots[item]
                one_end, two_end = starts[known], starts[ITEMS + known]
                begin = jnp.where(
                    q_spots >= two_end, two_end, jnp.where(q_spots >= one_end, one_end, 0)
                )
                k_spots = k_places + (word >> 20) * BLOCK
                value = jnp.where((k_spots <= q_spots) & (k_spots >= begin), value, NEG)
            held[slot, s] = value
            tops[slot, s] = jnp.max(value.reshape(STEP // 8, 8, LANES), axis=0)

    def absorb(table, at, slot):
        words = [table[at * UNITS + s] for s in range(UNITS)]
        items = [word & 63 for word in words]
        before = [peak[item] for item in items]
        now = []
        for s, old in enumerate(before):
            now.append(jnp.maximum(old, jnp.max(tops[slot, s], axis=0, keepdims=True)))
        fades = [jnp.exp2(old - new) for old, new in zip(before, now)]
        for item, new in zip(items, now):
            peak[item] = new
        added, updates = [], []
        for s, (word, new) in enumerate(zip(words, now)):
            weight = jnp.exp2(held[slot, s].reshape(STEP // 8, 8, LANES) - new[None])
            added.append(jnp.sum(weight, axis=0))
            updates.append(
                lax.dot_general(
                    fetch(word, slice(WIDTH, 2 * WIDTH)),
                    weight.reshape(STEP, LANES).astype(jnp.bfloat16),
                    (((0,), (0,)), ((), ())),
                    preferred_element_type=jnp.float32,
                )
            )
        totals = [total[item] for item in items]
        for item, old, fade, more in zip(items, totals, fades, added):
            total[item] = old * fade + more
        for item, fade, update in zip(items, fades, updates):
            kept = sums[item].reshape(WIDTH // 8, 8, LANES) * fade[None]
            sums[item] = kept.reshape(WIDTH, LANES) + update

    def run(table, turns, masked):
        score(table, 0, masked, 0)

        @pl.loop(0, (turns + 1) // 2)
        def _(pair):
            score(table, 2 * pair + 1, masked, 1)
            absorb(table, 2 * pair, 0)
            score(table, 2 * pair + 2, masked, 0)
            absorb(table, 2 * pair + 1, 1)

    run(table_m, meta[0], True)
    run(table_f, meta[1], False)

    sublane = lax.broadcasted_iota(jnp.int32, (8, WIDTH), 0)
    filler = jnp.zeros((8, 2 * WIDTH - LANES), jnp.float32)

    def finish(item):
        whole = jnp.sum(total[item], axis=0, keepdims=True)
        mean = sums[item] * (1.0 / whole)
        level = peak[item] + jnp.log2(whole)
        high = level.astype(jnp.bfloat16).astype(jnp.float32)
        middle = (level - high).astype(jnp.bfloat16).astype(jnp.float32)
        low = level - high - middle
        notes = jnp.zeros((8, WIDTH), jnp.float32)
        for at, piece in enumerate((high, middle, low)):
            left, right = piece[:, :WIDTH], jnp.concatenate([piece[:, WIDTH:], filler], axis=1)
            notes = jnp.where(sublane == 2 * at, left, notes)
            notes = jnp.where(sublane == 2 * at + 1, right, notes)
        block = jnp.concatenate([mean.T, notes, jnp.zeros_like(notes)], axis=0)
        o_ref[item] = block.astype(jnp.bfloat16)

    @pl.loop(0, ITEMS // 4)
    def _(at):
        for more in range(4):
            finish(at * 4 + more)


def attend(queries, keys_values, tables, half, part, plane, core):
    table_m, table_f, spots, starts, turns = tables
    meta = jnp.concatenate([turns, jnp.stack([half, part, plane, core])]).astype(jnp.int32)
    once = pl.Buffered(1)
    return pl.pallas_call(
        attend_kernel,
        out_shape=jax.ShapeDtypeStruct((ITEMS, PIECE, WIDTH), jnp.bfloat16),
        grid_spec=pltpu.PrefetchScalarGridSpec(
            num_scalar_prefetch=5,
            grid=(1,),
            in_specs=[
                pl.BlockSpec(queries.shape, lambda i, *_: (0, 0, 0), pipeline_mode=once),
            ]
            + [pl.BlockSpec(memory_space=pl.ANY)] * PARTS,
            out_specs=pl.BlockSpec((ITEMS, PIECE, WIDTH), lambda i, *_: (0, 0, 0)),
            scratch_shapes=[
                pltpu.VMEM((8, 32, RUN, 2 * WIDTH), jnp.bfloat16),
                pltpu.SemaphoreType.DMA((PARTS,)),
                pltpu.VMEM((2, UNITS, STEP, LANES), jnp.float32),
                pltpu.VMEM((2, UNITS, 8, LANES), jnp.float32),
                pltpu.VMEM((ITEMS + 1, 8, LANES), jnp.float32),
                pltpu.VMEM((ITEMS + 1, 8, LANES), jnp.float32),
                pltpu.VMEM((ITEMS + 1, WIDTH, LANES), jnp.float32),
            ],
        ),
        compiler_params=pltpu.CompilerParams(vmem_limit_bytes=48 * 1024 * 1024),
    )(table_m, table_f, spots, starts, meta, queries, *keys_values)


def join_kernel(got_ref, out_ref):
    for part in range(SPREAD):
        one = got_ref[0, 0, part].astype(jnp.float32)
        two = got_ref[0, 1, part].astype(jnp.float32)
        levels = [
            x[LANES : LANES + 2] + x[LANES + 2 : LANES + 4] + x[LANES + 4 : LANES + 6]
            for x in (one, two)
        ]
        ahead = levels[1] - levels[0]
        shares = jnp.concatenate(
            [1.0 / (1.0 + jnp.exp2(ahead)), 1.0 / (1.0 + jnp.exp2(-ahead))], axis=0
        )
        shares = jnp.concatenate([shares, shares], axis=0).T
        for head in range(HEADS):
            rows = slice(head * PART, (head + 1) * PART)
            at, column = head * PART % WIDTH, head * PART // WIDTH
            joined = one[rows] * shares[at : at + PART, column : column + 1]
            joined = joined + two[rows] * shares[at : at + PART, column + 2 : column + 3]
            out_ref[part * PART : (part + 1) * PART, head * WIDTH : (head + 1) * WIDTH] = (
                joined.astype(jnp.bfloat16)
            )


def join(got):
    return pl.pallas_call(
        join_kernel,
        out_shape=jax.ShapeDtypeStruct((HALF, 4 * HEADS * WIDTH), jnp.bfloat16),
        grid=(4,),
        in_specs=[pl.BlockSpec((1,) + got.shape[1:], lambda i: (i, 0, 0, 0, 0))],
        out_specs=pl.BlockSpec((HALF, HEADS * WIDTH), lambda i: (0, i)),
        compiler_params=pltpu.CompilerParams(vmem_limit_bytes=24 * 1024 * 1024),
    )(got)


def pack_queries_kernel(q_ref, out_ref):
    for part in range(SPREAD):
        for head in range(HEADS):
            block = q_ref[part * PART : (part + 1) * PART, head * WIDTH : (head + 1) * WIDTH]
            for half in range(2):
                out_ref[0, half, part, head * PART : (head + 1) * PART, :] = block


def pack_queries(queries):
    packed = pl.pallas_call(
        pack_queries_kernel,
        out_shape=jax.ShapeDtypeStruct((4, 2, SPREAD, LANES, WIDTH), queries.dtype),
        grid=(4,),
        in_specs=[pl.BlockSpec((HALF, HEADS * WIDTH), lambda i: (0, i))],
        out_specs=pl.BlockSpec((1, 2, SPREAD, LANES, WIDTH), lambda i: (i, 0, 0, 0, 0)),
    )(queries)
    return packed.reshape(32, LANES, WIDTH)


def pack_keys_kernel(k_ref, v_ref, out_ref):
    for head in range(4):
        columns = slice(head * WIDTH, (head + 1) * WIDTH)
        for half in range(2):
            rows = slice(half * RUN, (half + 1) * RUN)
            for part in range(SPREAD):
                out_ref[head, half, part, :, :WIDTH] = k_ref[rows, columns]
                out_ref[head, half, part, :, WIDTH:] = v_ref[rows, columns]


def pack_keys(keys, values):
    packed = pl.pallas_call(
        pack_keys_kernel,
        out_shape=jax.ShapeDtypeStruct((4, 2, SPREAD, RUN, 2 * WIDTH), keys.dtype),
    )(keys, values)
    return packed.reshape(32, RUN, 2 * WIDTH)


def gather_planes(kv, core, tables, pieces):
    def device(member, plane):
        return ((plane // 4) * 32 + member) * 4 + plane % 4

    every = [(member, plane) for member in range(32) for plane in range(8)]
    onward = [(device(m, z), device(m, (z + 1 - 2 * (m % 2)) % 8)) for m, z in every]
    swap = [(device(m, z), device(m ^ 1, z)) for m, z in every]
    first = lax.ppermute(kv, ALL, onward)
    first, tables, pieces = lax.optimization_barrier((first, tables, pieces))
    second = lax.ppermute(first, ALL, onward)
    first_swapped = lax.ppermute(first, ALL, swap)
    got = lax.all_to_all(pieces, "seq", split_axis=0, concat_axis=0, tiled=True)
    third = lax.ppermute(second, ALL, onward)
    third, got = lax.optimization_barrier((third, got))
    second_swapped = lax.ppermute(second, ALL, swap)
    last = lax.ppermute(lax.dynamic_slice_in_dim(third, core * 16, 16, 0), ALL, onward)
    third_swapped = lax.ppermute(third, ALL, swap)
    last_swapped = lax.ppermute(last, ALL, swap)
    parts = [kv, first, first_swapped, second, second_swapped]
    return parts + [third, third_swapped, last, last_swapped], tables, got


def body(queries, keys, values, doc_lengths, block_order):
    member = lax.axis_index("seq")
    half, part, core = (member // SPREAD) % 2, member % SPREAD, member % 2
    plane = lax.axis_index("dp") * 4 + lax.axis_index("head")

    kv = lax.all_to_all(
        pack_keys(keys, values), "seq", split_axis=0, concat_axis=0, tiled=True
    )
    tables = plan(doc_lengths, block_order, lax.axis_index("dp"), lax.axis_index("head"))
    keys_values, tables, got = gather_planes(kv, core, tables, pack_queries(queries))
    out = attend(got, keys_values, tables, half, part, plane, core)
    home = lax.all_to_all(out, "seq", split_axis=0, concat_axis=0, tiled=True)
    return join(home.reshape(4, 2, SPREAD, PIECE, WIDTH))


def solution(mesh):
    rows = P(ALL, None)
    return jax.shard_map(
        body,
        mesh=mesh,
        in_specs=(rows, rows, rows, P(), P()),
        out_specs=rows,
        check_vma=False,
    )
```
